512 devices in a mesh: seq: 32 (over z, x_lo), tp: 16 (over x_hi, y, core).
Axes of the slice: x: 4 (x_hi: 2, x_lo: 2; x = x_hi * 2 + x_lo), y: 4, z: 16, core: 2. Of those that a mesh axis runs over, the one named last changes fastest.
Arguments:
- tokens: bfloat16 [256, 8192], P('tp', 'seq'), may hold values from -6 to 6
- grad_out: bfloat16 [256, 8192], P('tp', 'seq'), may hold values from -6 to 6
- gate_values: bfloat16 [8192, 28672], P('seq', 'tp'), may hold values from -0.0625 to 0.0625
- up_values: bfloat16 [8192, 28672], P('seq', 'tp'), may hold values from -0.0625 to 0.0625
- down_values: bfloat16 [28672, 8192], P('tp', 'seq'), may hold values from -0.03125 to 0.03125
- gate_scales: float32 [64, 224], P('seq', 'tp'), may hold values from 0.5 to 2
- up_scales: float32 [64, 224], P('seq', 'tp'), may hold values from 0.5 to 2
- down_scales: float32 [224, 64], P('tp', 'seq'), may hold values from 0.5 to 2
Outputs:
- mixed: bfloat16 [256, 8192], P('tp', 'seq')
- input_grad: bfloat16 [256, 8192], P('tp', 'seq')
The draws below stay inside these ranges and needn't reach their ends.
All inputs are finite; a program needn't handle non-finite values.
Results may differ from the reference program's by a relative error of at most 0.0072.
Values may be sent and summed in bfloat16 or wider, within the bound.
No kernel may reach another device: no remote copies, remote signals or barrier semaphores. Data moves between devices by JAX's collectives and lax.ppermute only.
A program may use at most 64 MiB of HBM per device.

```python
import math
import jax
import jax.numpy as jnp

D = 8192
FF = 28672
BLK = 128
TOK = 256


def steps_of(key, dims, shards, smallest, largest):
    def one(dim, blocks):
        steps = jax.random.uniform(jax.random.fold_in(jax.random.fold_in(key, 6), dim), (blocks,), jnp.float32, smallest / len(shards), largest / len(shards))
        return jnp.repeat(jnp.exp(steps), dims[dim] // blocks).reshape((-1,) + (1,) * (len(dims) - dim - 1))

    loudness = one(*shards[0])
    for cut in shards[1:]:
        loudness = loudness * one(*cut)
    return loudness


def normal_values(key, extent, scale, reach, split=(), held_as=jnp.bfloat16):
    gain = steps_of(key, extent, split, -0.22, 0.18) if split else 1.0
    array = jax.random.normal(key, extent, jnp.float32) * scale * gain
    return jnp.minimum(jnp.maximum(array, -reach), reach).astype(held_as)


def setup_inputs(seed: int = 0) -> dict:
    key_list = jax.random.split(jax.random.key(seed), 9)
    tokens = normal_values(key_list[0], (TOK, D), 1.0, 6.0, ((0, 16), (1, 32)))
    grad_out = normal_values(key_list[1], (TOK, D), 1.0, 6.0, ((0, 16), (1, 32)))
    gate_values = normal_values(key_list[2], (D, FF), D ** -0.5, 0.0625, ((0, 32), (1, 16)))
    up_values = normal_values(key_list[3], (D, FF), D ** -0.5, 0.0625, ((0, 32), (1, 16)))
    down_values = normal_values(key_list[4], (FF, D), FF ** -0.5, 0.03125, ((0, 16), (1, 32)))
    gate_scales = jnp.clip(jnp.exp(math.log(2.0) - 1.3862944 * jax.random.uniform(key_list[5], (D // BLK, FF // BLK), jnp.float32) ** steps_of(key_list[5], (D // BLK, FF // BLK), ((0, 32), (1, 16)), -0.2, 0.2)), 0.5, 2.0)
    up_scales = jnp.clip(jnp.exp(math.log(2.0) - 1.3862944 * jax.random.uniform(key_list[6], (D // BLK, FF // BLK), jnp.float32) ** steps_of(key_list[6], (D // BLK, FF // BLK), ((0, 32), (1, 16)), -0.2, 0.2)), 0.5, 2.0)
    down_scales = jnp.clip(jnp.exp(math.log(2.0) - 1.3862944 * jax.random.uniform(key_list[7], (FF // BLK, D // BLK), jnp.float32) ** steps_of(key_list[7], (FF // BLK, D // BLK), ((0, 16), (1, 32)), -0.2, 0.2)), 0.5, 2.0)
    return dict(tokens=tokens, grad_out=grad_out, gate_values=gate_values, up_values=up_values, down_values=down_values, gate_scales=gate_scales, up_scales=up_scales, down_scales=down_scales)


def dequantize(values, scales):
    spread = jnp.repeat(jnp.repeat(scales, BLK, axis=0), BLK, axis=1)
    return (values.astype(jnp.float32) * spread).astype(jnp.bfloat16)


def gated_unit(gate_sum, up_sum, back_sum):
    sig = jax.nn.sigmoid(gate_sum)
    active = gate_sum * sig
    hidden = (active * up_sum).astype(jnp.bfloat16)
    gate_grad = (back_sum * up_sum * (sig * (1.0 + gate_sum * (1.0 - sig)))).astype(jnp.bfloat16)
    up_grad = (back_sum * active).astype(jnp.bfloat16)
    return hidden, gate_grad, up_grad


def reference(tokens, grad_out, gate_values, up_values, down_values, gate_scales, up_scales, down_scales):
    w_gate = dequantize(gate_values, gate_scales)
    w_up = dequantize(up_values, up_scales)
    w_down = dequantize(down_values, down_scales)
    gate_sum = jnp.dot(tokens, w_gate, preferred_element_type=jnp.float32)
    up_sum = jnp.dot(tokens, w_up, preferred_element_type=jnp.float32)
    back_sum = jnp.dot(grad_out, w_down.T, preferred_element_type=jnp.float32)
    hidden, gate_grad, up_grad = gated_unit(gate_sum, up_sum, back_sum)
    mixed = jnp.dot(hidden, w_down, preferred_element_type=jnp.float32).astype(jnp.bfloat16)
    input_grad = jnp.dot(gate_grad, w_gate.T, preferred_element_type=jnp.float32) + jnp.dot(up_grad, w_up.T, preferred_element_type=jnp.float32)
    return mixed, input_grad.astype(jnp.bfloat16)
```

```python
import functools

import jax
import jax.numpy as jnp
from jax import lax
from jax.experimental import pallas as pl
from jax.experimental.pallas import tpu as pltpu
from jax.sharding import Mesh, PartitionSpec as P

BLK = 128
Z = ("zh", "zl")
TP = ("xh", "y", "core")
SEQ = ("zh", "zl", "xl")
F32, BF16 = jnp.float32, jnp.bfloat16
PARAMS = pltpu.CompilerParams(vmem_limit_bytes=24 * 1024 * 1024)
VMEM = pl.BlockSpec(memory_space=pltpu.VMEM)
SMEM = pl.BlockSpec(memory_space=pltpu.SMEM)


def call(body, out_shapes, ins, name, smem=0, scratch=()):
    return pl.pallas_call(
        body,
        out_shape=[jax.ShapeDtypeStruct(s, d) for s, d in out_shapes],
        in_specs=[SMEM] * smem + [VMEM] * (len(ins) - smem),
        out_specs=[VMEM] * len(out_shapes),
        scratch_shapes=list(scratch),
        compiler_params=PARAMS,
        name=name,
    )(*ins)


def scaled(ref, rows, cols, scale):
    return (ref[rows, cols].astype(F32) * scale).astype(BF16)


def dequant_kernel(pos, gs, us, ds, gate, up, down, gu_keep, gu_send, d_keep, d_send):
    depth, cols = gu_keep.shape[0] // 2, gu_keep.shape[1]
    blocks = cols // BLK
    for which, gu_out, d_out in ((pos[0], gu_keep, d_keep), (1 - pos[0], gu_send, d_send)):
        for j in range(blocks):
            src = which * blocks + j
            at = pl.ds(pl.multiple_of(src * BLK, BLK), BLK)
            for i in range(depth // BLK):
                rows = slice(i * BLK, (i + 1) * BLK)
                low = slice(depth + i * BLK, depth + (i + 1) * BLK)
                to = slice(j * BLK, (j + 1) * BLK)
                gu_out[rows, to] = scaled(gate, rows, at, gs[i, src])
                gu_out[low, to] = scaled(up, rows, at, us[i, src])
                d_out[to, rows] = scaled(down, at, rows, ds[src, i])


def nt(a, b):
    return lax.dot_general(a, b, (((1,), (1,)), ((), ())), preferred_element_type=F32)


def nn(a, b):
    return jnp.dot(a, b, preferred_element_type=F32)


def partial_kernel(pos, acts, gu_keep, gu_other, d_keep, d_other, plus1, minus1, plus2, minus2, own):
    xl, zl = pos[0], pos[1]
    depth = d_keep.shape[1]
    for shift, out in ((1, plus1), (3, minus1), (2, None), (0, own)):
        cls = lax.rem(zl + shift, 4)

        def rows(x, which):
            return jnp.concatenate([acts[x, ch * 4 + cls, which] for ch in range(4)], axis=0)

        tm, to = rows(xl, 0), rows(1 - xl, 0)
        gm, go = rows(xl, 1), rows(1 - xl, 1)
        parts = (
            nn(tm, gu_keep[:depth]) + nn(to, gu_other[:depth]),
            nn(tm, gu_keep[depth:]) + nn(to, gu_other[depth:]),
            nt(gm, d_keep[...]) + nt(go, d_other[...]),
        )
        for k, part in enumerate(parts):
            width = part.shape[1]
            cols = slice(k * width, (k + 1) * width)
            if out is None:
                half = part.shape[0] // 2
                plus2[:, cols] = part[:half].astype(BF16)
                minus2[:, cols] = part[half:].astype(BF16)
            else:
                out[:, cols] = part.astype(out.dtype)


def window_kernel(own, a1, b1, a2, b2, out):
    half = a2.shape[0]
    for rows, far in ((slice(0, half), a2), (slice(half, 2 * half), b2)):
        total = own[rows, :] + a1[rows, :].astype(F32) + b1[rows, :].astype(F32) + far[...].astype(F32)
        for ch in range(2):
            block = rows.start // 16 + ch
            out[block] = total[ch * 16 : (ch + 1) * 16].astype(BF16)


def gated_kernel(parts, out):
    width = parts.shape[2] // 3

    def total(k):
        cols = slice(k * width, (k + 1) * width)
        s = parts[0, :, cols].astype(F32)
        for i in range(1, parts.shape[0]):
            s = s + parts[i, :, cols].astype(F32)
        return s

    gate_sum, up_sum, back_sum = total(0), total(1), total(2)
    sig = jax.nn.sigmoid(gate_sum)
    active = gate_sum * sig
    results = (
        active * up_sum,
        back_sum * up_sum * (sig * (1.0 + gate_sum * (1.0 - sig))),
        back_sum * active,
    )
    for k, result in enumerate(results):
        for i in range(out.shape[0]):
            out[i, :, k * width : (k + 1) * width] = result.astype(BF16)


def output_kernel(pos, own, a1, b1, a2, b2, gu_keep, gu_other, d_keep, d_other, out, rows):
    xl, zl = pos[0], pos[1]
    n, half = own.shape[0], a2.shape[0]
    width = d_keep.shape[0]
    depth = d_keep.shape[1]
    rows[0:n] = own[...]
    rows[n : 2 * n] = a1[...]
    rows[2 * n : 2 * n + half] = a2[...]
    rows[2 * n + half : 3 * n] = b2[...]
    rows[3 * n : 4 * n] = b1[...]
    hidden, gate_grad, up_grad = (rows[:, k * width : (k + 1) * width] for k in range(3))
    for x, gu, d in ((xl, gu_keep, d_keep), (1 - xl, gu_other, d_other)):
        mixed = nn(hidden, d[...]).astype(BF16)
        grad = (nt(gate_grad, gu[:depth]) + nt(up_grad, gu[depth:])).astype(BF16)
        for order, shift in enumerate((0, 3, 2, 1)):
            cls = lax.rem(zl + shift, 4)
            for ch in range(4):
                at = slice(order * n + ch * 16, order * n + (ch + 1) * 16)
                out[x, ch * 4 + cls, :, 0:depth] = mixed[at]
                out[x, ch * 4 + cls, :, depth : 2 * depth] = grad[at]


def sum_kernel(parts, mixed, grad):
    depth = mixed.shape[1]
    total = parts[0].astype(F32)
    for i in range(1, parts.shape[0]):
        total = total + parts[i].astype(F32)
    mixed[...] = total[:, :depth].astype(BF16)
    grad[...] = total[:, depth:].astype(BF16)


def along_z(x, shift):
    return lax.ppermute(x, Z, [(i, (i + shift) % 16) for i in range(16)])


def swap(x):
    return lax.ppermute(x, "xl", [(0, 1), (1, 0)])


def shards(tokens, grad_out, gate, up, down, gate_scales, up_scales, down_scales):
    n_tok, depth = tokens.shape
    width = gate.shape[1] // 2
    pos = jnp.stack([lax.axis_index("xl"), lax.axis_index("zl")]).astype(jnp.int32)
    both = jnp.stack([tokens, grad_out])
    acts = lax.all_to_all(
        jnp.broadcast_to(both[None], (32,) + both.shape), ("xl",) + TP, 0, 0, tiled=True
    ).reshape(2, 16, 2, n_tok, depth)
    gu_keep, gu_send, d_keep, d_send = call(
        dequant_kernel,
        [((2 * depth, width), BF16)] * 2 + [((width, depth), BF16)] * 2,
        (pos, gate_scales, up_scales, down_scales, gate, up, down),
        "dequant",
        smem=4,
    )
    d_other, gu_other = swap(d_send), swap(gu_send)
    n, all_cols = 4 * n_tok, 3 * width
    plus1, minus1, plus2, minus2, own = call(
        partial_kernel,
        [((n, all_cols), BF16)] * 2 + [((n // 2, all_cols), BF16)] * 2 + [((n, all_cols), F32)],
        (pos, acts, gu_keep, gu_other, d_keep, d_other),
        "partials",
        smem=1,
    )
    a1, b1 = along_z(plus1, 1), along_z(minus1, -1)
    a2, b2 = along_z(plus2, 2), along_z(minus2, -2)
    (window,) = call(window_kernel, [((4, n_tok, all_cols), BF16)], (own, a1, b1, a2, b2), "window")
    (spread,) = call(
        gated_kernel,
        [((4, n_tok, all_cols), BF16)],
        (lax.all_to_all(window, "zh", 0, 0, tiled=True),),
        "gated",
    )
    mine = lax.all_to_all(spread, "zh", 0, 0, tiled=True).reshape(n, all_cols)
    a1, b1 = along_z(mine, 1), along_z(mine, -1)
    a2, b2 = along_z(mine[: n // 2], 2), along_z(mine[n // 2 :], -2)
    (shares,) = call(
        output_kernel,
        [((2, 16, n_tok, 2 * depth), BF16)],
        (pos, mine, a1, b1, a2, b2, gu_keep, gu_other, d_keep, d_other),
        "outputs",
        smem=1,
        scratch=[pltpu.VMEM((4 * n, all_cols), BF16)],
    )
    gathered = lax.all_to_all(
        shares.reshape(32, n_tok, 2 * depth), ("xl",) + TP, 0, 0, tiled=True
    )
    return tuple(
        call(sum_kernel, [((n_tok, depth), BF16)] * 2, (gathered,), "sums")
    )


def solution(mesh):
    fine = Mesh(mesh.devices.reshape(4, 4, 2, 2, 4, 2), ("zh", "zl", "xl", "xh", "y", "core"))
    weights, acts = P(SEQ, TP), P(TP, SEQ)
    return jax.shard_map(
        shards,
        mesh=fine,
        in_specs=(acts, acts, weights, weights, acts, weights, weights, acts),
        out_specs=(acts, acts),
        check_vma=False,
    )
```

```python
import functools

import jax
import jax.numpy as jnp
from jax import lax
from jax.experimental import pallas as pl
from jax.experimental.pallas import tpu as pltpu
from jax.sharding import Mesh, PartitionSpec as P

BLK = 128
Z = ("zh", "zl")
TP = ("xh", "y", "core")
SEQ = ("zh", "zl", "xl")
F32, BF16 = jnp.float32, jnp.bfloat16
VMEM = pl.BlockSpec(memory_space=pltpu.VMEM)
SMEM = pl.BlockSpec(memory_space=pltpu.SMEM)
ANY = pl.BlockSpec(memory_space=pl.ANY)


def call(body, out_shapes, ins, name, specs=None, scratch=(), limit=16):
    return pl.pallas_call(
        body,
        out_shape=[jax.ShapeDtypeStruct(s, d) for s, d in out_shapes],
        in_specs=specs or [VMEM] * len(ins),
        out_specs=[VMEM] * len(out_shapes),
        scratch_shapes=list(scratch),
        compiler_params=pltpu.CompilerParams(vmem_limit_bytes=limit * 1024 * 1024),
        name=name,
    )(*ins)


def scale_kernel(kept, chunks, repeats, *refs):
    scales, (gate, up, down) = refs[:3], refs[3:6]
    outs, (g_buf, u_buf, d_buf), tables = refs[6:-7], refs[-7:-4], refs[-4:-1]
    sems = refs[-1]
    depth = g_buf.shape[0]
    half = gate.shape[1] // (2 * BLK)
    xl = lax.axis_index("xl")
    start = (xl if kept else 1 - xl) * half
    lo, count = chunks[0][0], sum(c for _, c in chunks)
    at = pl.ds(pl.multiple_of((start + lo) * BLK, BLK), count * BLK)
    pairs = [(down.at[at, :], d_buf), (gate.at[:, at], g_buf), (up.at[:, at], u_buf)]
    pairs = list(zip(scales, tables)) + pairs
    copies = [pltpu.make_async_copy(a, b, sems.at[i]) for i, (a, b) in enumerate(pairs)]
    for copy in copies[3:] + copies[:3]:
        copy.start()
    for copy in copies[:3]:
        copy.wait()
    gs, us, ds = tables
    for which, copy in enumerate(copies[3:]):
        copy.wait()
        for (first, n), *out in zip(chunks, *(outs[r * len(chunks) :] for r in range(repeats))):
            for j in range(first, first + n):
                src = slice((j - lo) * BLK, (j - lo + 1) * BLK)
                cols = slice((j - first) * BLK, (j - first + 1) * BLK)
                for i in range(depth // BLK):
                    rows = slice(i * BLK, (i + 1) * BLK)
                    if which == 0:
                        to = slice(2 * depth + i * BLK, 2 * depth + (i + 1) * BLK)
                        value = (d_buf[src, rows].astype(F32) * ds[i, start + j]).T
                    elif which == 1:
                        to = rows
                        value = g_buf[rows, src].astype(F32) * gs[i, start + j]
                    else:
                        to = slice(depth + i * BLK, depth + (i + 1) * BLK)
                        value = u_buf[rows, src].astype(F32) * us[i, start + j]
                    for ref in out:
                        ref[to, cols] = value.astype(BF16)


def nt(a, b):
    return lax.dot_general(a, b, (((1,), (1,)), ((), ())), preferred_element_type=F32)


def nn(a, b):
    return jnp.dot(a, b, preferred_element_type=F32)


def toward():
    return 1 - 2 * lax.axis_index("core")


def partial_kernel(width, acts, keep_in, other_in, *refs):
    ahead, behind, far, own, keep, other, sems = refs[-7:]
    copies = [
        pltpu.make_async_copy(keep_in, keep, sems.at[0]),
        pltpu.make_async_copy(other_in, other, sems.at[1]),
    ]
    for copy in copies:
        copy.start()
    for copy in copies:
        copy.wait()
    xl, zl, turn = lax.axis_index("xl"), lax.axis_index("zl"), toward()
    depth = keep.shape[0] // 3
    for shift, out in ((turn, ahead), (-turn, behind), (2, far), (0, own)):
        cls = lax.rem(zl + shift + 4, 4)

        def rows(x, which):
            return jnp.concatenate([acts[x, ch * 4 + cls, which] for ch in range(4)], axis=0)

        for which, ks in ((0, (0, 1)), (1, (2,))):
            mine, his = rows(xl, which), rows(1 - xl, which)
            for k in ks:
                w = slice(k * depth, (k + 1) * depth)
                part = nn(mine, keep[w]) + nn(his, other[w])
                out[:, k * width : (k + 1) * width] = part.astype(out.dtype)


def window_kernel(*refs):
    out, left = refs[-1], 0
    n = out.shape[1]
    for k in range(0, len(refs) - 1, 4):
        own, *parts = refs[k : k + 4]
        width = own.shape[1]
        for i in range(out.shape[0]):
            rows = slice(i * n, (i + 1) * n)
            total = own[rows, :]
            for part in parts:
                total = total + part[rows, :].astype(F32)
            out[i, :, left : left + width] = total.astype(BF16)
        left += width


def spans(widths):
    left, at = 0, []
    for w in widths:
        at.append([slice(left + k * w, left + (k + 1) * w) for k in range(3)])
        left += 3 * w
    return at


def gated_kernel(widths, parts, out):
    def total(cols):
        s = parts[0, :, cols].astype(F32)
        for i in range(1, parts.shape[0]):
            s = s + parts[i, :, cols].astype(F32)
        return s

    for at in spans(widths):
        gate_sum, up_sum, back_sum = (total(cols) for cols in at)
        sig = jax.nn.sigmoid(gate_sum)
        active = gate_sum * sig
        results = (
            active * up_sum,
            back_sum * up_sum * (sig * (1.0 + gate_sum * (1.0 - sig))),
            back_sum * active,
        )
        for cols, result in zip(at, results):
            for i in range(out.shape[0]):
                out[i, :, cols] = result.astype(BF16)


def output_kernel(widths, own, ahead, behind, far, *refs):
    weights, out, rows = refs[:-2], refs[-2], refs[-1]
    xl, zl, turn = lax.axis_index("xl"), lax.axis_index("zl"), toward()
    n = out.shape[1] // 16
    depth = weights[0].shape[0] // 3
    for shift, src in ((0, own), (-turn, ahead), (turn, behind), (2, far)):
        cls = lax.rem(zl + shift + 4, 4)
        for i in range(4):
            at = pl.ds(pl.multiple_of((i * 4 + cls) * n, n), n)
            rows[at, :] = src[i * n : (i + 1) * n, :]
    for k, x in enumerate((xl, 1 - xl)):
        mixed = grad = 0.0
        for c, at in enumerate(spans(widths)):
            w = weights[2 * c + k]
            hidden, gate_grad, up_grad = (rows[:, cols] for cols in at)
            mixed = mixed + nt(hidden, w[2 * depth :])
            grad = grad + nt(gate_grad, w[:depth]) + nt(up_grad, w[depth : 2 * depth])
        out[x, :, 0:depth] = mixed.astype(BF16)
        out[x, :, depth : 2 * depth] = grad.astype(BF16)


def sum_kernel(parts, mixed, grad):
    depth = mixed.shape[1]
    total = parts[0].astype(F32)
    for i in range(1, parts.shape[0]):
        total = total + parts[i].astype(F32)
    mixed[...] = total[:, :depth].astype(BF16)
    grad[...] = total[:, depth:].astype(BF16)


def along_z(x, shift):
    pairs = [(2 * z + c, 2 * ((z + shift * (1 - 2 * c)) % 16) + c) for z in range(16) for c in range(2)]
    return lax.ppermute(x, Z + ("core",), pairs)


def exchange(x):
    return tuple(along_z(x[i], shift) for i, shift in enumerate((1, -1, 2)))


def shards(tokens, grad_out, gate, up, down, gate_scales, up_scales, down_scales):
    n_tok, depth = tokens.shape
    half = gate.shape[1] // (2 * BLK)
    chunks = ((0, (half + 1) // 2), ((half + 1) // 2, half // 2))

    def scaled(kept, chunks, limit, copies=1):
        w = sum(count for _, count in chunks) * BLK
        outs = call(
            functools.partial(scale_kernel, kept, chunks, copies),
            [((3 * depth, count * BLK), BF16) for _, count in chunks] * copies,
            (gate_scales, up_scales, down_scales.T, gate, up, down),
            "scaled",
            specs=[ANY] * 6,
            scratch=[pltpu.VMEM((depth, w), BF16)] * 2
            + [pltpu.VMEM((w, depth), BF16)]
            + [pltpu.SMEM(gate_scales.shape, F32)] * 3
            + [pltpu.SemaphoreType.DMA((6,))],
            limit=limit,
        )
        return outs[: len(chunks)], outs[len(chunks) :]

    def swap(x):
        return lax.ppermute(x, "xl", [(0, 1), (1, 0)])

    (first, second), _ = scaled(False, chunks, 60)
    keeps, _ = scaled(True, chunks, 60)
    first_other = swap(first)
    second, tokens, grad_out = lax.optimization_barrier((second, tokens, grad_out))
    acts = jnp.stack([tokens, grad_out])
    acts = lax.all_to_all(
        jnp.broadcast_to(acts[None], (32,) + acts.shape), ("xl",) + TP, 0, 0, tiled=True
    ).reshape(2, 16, 2, n_tok, depth)
    first_other, second, keeps = lax.optimization_barrier((first_other, second, keeps))
    others = (first_other, swap(second))

    n = 4 * n_tok
    widths = tuple(count * BLK for _, count in chunks)
    w = 3 * sum(widths)
    weights, windows = [], []
    for keep, other, width in zip(keeps, others, widths):
        ins = (acts, keep, other, *windows[1:2])
        *parts, own = call(
            functools.partial(partial_kernel, width),
            [((n, 3 * width), BF16)] * 3 + [((n, 3 * width), F32)],
            ins,
            "partials",
            specs=[VMEM] + [ANY] * (len(ins) - 1),
            scratch=[pltpu.VMEM(keep.shape, BF16)] * 2 + [pltpu.SemaphoreType.DMA((2,))],
        )
        windows += [own, *exchange(parts)]
        weights += [keep, other]
    (window,) = call(window_kernel, [((4, n_tok, w), BF16)], windows, "window")
    (spread,) = call(
        functools.partial(gated_kernel, widths),
        [((4, n_tok, w), BF16)],
        (lax.all_to_all(window, "zh", 0, 0, tiled=True),),
        "gated",
    )
    mine = lax.all_to_all(spread, "zh", 0, 0, tiled=True).reshape(n, w)
    (shares,) = call(
        functools.partial(output_kernel, widths),
        [((2, 16 * n_tok, 2 * depth), BF16)],
        (mine, *exchange([mine] * 3), *weights),
        "outputs",
        scratch=[pltpu.VMEM((4 * n, w), BF16)],
    )
    gathered = lax.all_to_all(
        shares.reshape(32, n_tok, 2 * depth), ("xl",) + TP, 0, 0, tiled=True
    )
    return tuple(call(sum_kernel, [((n_tok, depth), BF16)] * 2, (gathered,), "sums"))


def solution(mesh):
    fine = Mesh(mesh.devices.reshape(4, 4, 2, 2, 4, 2), ("zh", "zl", "xl", "xh", "y", "core"))
    weights, acts = P(SEQ, TP), P(TP, SEQ)
    return jax.shard_map(
        shards,
        mesh=fine,
        in_specs=(acts, acts, weights, weights, acts, weights, weights, acts),
        out_specs=(acts, acts),
        check_vma=False,
    )
```

```python
import functools

import jax
import jax.numpy as jnp
from jax import lax
from jax.experimental import pallas as pl
from jax.experimental.pallas import tpu as pltpu
from jax.sharding import Mesh, PartitionSpec as P

BLK = 128
Z = ("zh", "zl")
TP = ("xh", "y", "core")
SEQ = ("zh", "zl", "xl")
F32, BF16 = jnp.float32, jnp.bfloat16
VMEM = pl.BlockSpec(memory_space=pltpu.VMEM)
SMEM = pl.BlockSpec(memory_space=pltpu.SMEM)
ANY = pl.BlockSpec(memory_space=pl.ANY)


def call(body, out_shapes, ins, name, specs=None, scratch=(), limit=16):
    return pl.pallas_call(
        body,
        out_shape=[jax.ShapeDtypeStruct(s, d) for s, d in out_shapes],
        in_specs=specs or [VMEM] * len(ins),
        out_specs=[VMEM] * len(out_shapes),
        scratch_shapes=list(scratch),
        compiler_params=pltpu.CompilerParams(vmem_limit_bytes=limit * 1024 * 1024),
        name=name,
    )(*ins)


def scale_kernel(kept, chunks, repeats, *refs):
    scales, (gate, up, down) = refs[:3], refs[3:6]
    outs, (g_buf, u_buf, d_buf), tables = refs[6:-7], refs[-7:-4], refs[-4:-1]
    sems = refs[-1]
    depth = g_buf.shape[0]
    half = gate.shape[1] // (2 * BLK)
    xl = lax.axis_index("xl")
    start = (xl if kept else 1 - xl) * half
    lo, count = chunks[0][0], sum(c for _, c in chunks)
    at = pl.ds(pl.multiple_of((start + lo) * BLK, BLK), count * BLK)
    pairs = [(down.at[at, :], d_buf), (gate.at[:, at], g_buf), (up.at[:, at], u_buf)]
    pairs = list(zip(scales, tables)) + pairs
    copies = [pltpu.make_async_copy(a, b, sems.at[i]) for i, (a, b) in enumerate(pairs)]
    for copy in copies[3:] + copies[:3]:
        copy.start()
    for copy in copies[:3]:
        copy.wait()
    gs, us, ds = tables
    for which, copy in enumerate(copies[3:]):
        copy.wait()
        for (first, n), *out in zip(chunks, *(outs[r * len(chunks) :] for r in range(repeats))):
            for j in range(first, first + n):
                src = slice((j - lo) * BLK, (j - lo + 1) * BLK)
                cols = slice((j - first) * BLK, (j - first + 1) * BLK)
                for i in range(depth // BLK):
                    rows = slice(i * BLK, (i + 1) * BLK)
                    if which == 0:
                        to = slice(2 * depth + i * BLK, 2 * depth + (i + 1) * BLK)
                        value = (d_buf[src, rows].astype(F32) * ds[i, start + j]).T
                    elif which == 1:
                        to = rows
                        value = g_buf[rows, src].astype(F32) * gs[i, start + j]
                    else:
                        to = slice(depth + i * BLK, depth + (i + 1) * BLK)
                        value = u_buf[rows, src].astype(F32) * us[i, start + j]
                    for ref in out:
                        ref[to, cols] = value.astype(BF16)


def nt(a, b):
    return lax.dot_general(a, b, (((1,), (1,)), ((), ())), preferred_element_type=F32)


def nn(a, b):
    return jnp.dot(a, b, preferred_element_type=F32)


def toward():
    return 1 - 2 * lax.axis_index("core")


def partial_kernel(width, acts, keep_in, other_in, *refs):
    ahead, behind, far, own, keep, other, sems = refs[-7:]
    copies = [
        pltpu.make_async_copy(keep_in, keep, sems.at[0]),
        pltpu.make_async_copy(other_in, other, sems.at[1]),
    ]
    for copy in copies:
        copy.start()
    for copy in copies:
        copy.wait()
    xl, zl, turn = lax.axis_index("xl"), lax.axis_index("zl"), toward()
    depth = keep.shape[0] // 3
    for shift, out in ((turn, ahead), (-turn, behind), (2, far), (0, own)):
        cls = lax.rem(zl + shift + 4, 4)

        def rows(x, which):
            return jnp.concatenate([acts[x, ch * 4 + cls, which] for ch in range(4)], axis=0)

        for which, ks in ((0, (0, 1)), (1, (2,))):
            mine, his = rows(xl, which), rows(1 - xl, which)
            for k in ks:
                w = slice(k * depth, (k + 1) * depth)
                part = nn(mine, keep[w]) + nn(his, other[w])
                out[:, k * width : (k + 1) * width] = part.astype(out.dtype)


def window_kernel(*refs):
    here, ahead, far, behind, buf = refs[-5:]
    zh, turn = lax.axis_index("zh"), toward()
    n, left = here.shape[0], 0
    for k in range(0, len(refs) - 5, 4):
        own, *parts = refs[k : k + 4]
        total = own[...]
        for part in parts:
            total = total + part[...].astype(F32)
        buf[:, left : left + own.shape[1]] = total
        left += own.shape[1]
    for shift, out in ((2, far), (-turn, behind), (turn, ahead), (0, here)):
        at = pl.ds(pl.multiple_of(lax.rem(zh + shift + 4, 4) * n, n), n)
        out[...] = buf[at, :].astype(out.dtype)


def spans(widths):
    left, at = 0, []
    for w in widths:
        at.append([slice(left + k * w, left + (k + 1) * w) for k in range(3)])
        left += 3 * w
    return at


def gated_kernel(widths, here, direct, passed, out):
    def total(cols):
        return here[:, cols] + direct[:, cols].astype(F32) + passed[:, cols].astype(F32)

    for at in spans(widths):
        gate_sum, up_sum, back_sum = (total(cols) for cols in at)
        sig = jax.nn.sigmoid(gate_sum)
        active = gate_sum * sig
        results = (
            active * up_sum,
            back_sum * up_sum * (sig * (1.0 + gate_sum * (1.0 - sig))),
            back_sum * active,
        )
        for cols, result in zip(at, results):
            out[:, cols] = result.astype(BF16)


def output_kernel(widths, own, ahead, behind, far, *refs):
    weights, out, rows = refs[:-2], refs[-2], refs[-1]
    xl, turn = lax.axis_index("xl"), toward()
    z = lax.axis_index("zh") * 4 + lax.axis_index("zl")
    n = out.shape[1] // 16
    depth = weights[0].shape[0] // 3
    for shift, src in ((0, own), (-turn, ahead), (turn, behind), (-2 * turn, far)):
        sender = lax.rem(z + shift + 16, 16)
        for i, step in enumerate((0, -turn, 2, turn)):
            block = lax.rem(lax.div(sender, 4) + step + 4, 4) * 4 + lax.rem(sender, 4)
            at = pl.ds(pl.multiple_of(block * n, n), n)
            rows[at, :] = src[i * n : (i + 1) * n, :]
    for k, x in enumerate((xl, 1 - xl)):
        mixed = grad = 0.0
        for c, at in enumerate(spans(widths)):
            w = weights[2 * c + k]
            hidden, gate_grad, up_grad = (rows[:, cols] for cols in at)
            mixed = mixed + nt(hidden, w[2 * depth :])
            grad = grad + nt(gate_grad, w[:depth]) + nt(up_grad, w[depth : 2 * depth])
        out[x, :, 0:depth] = mixed.astype(BF16)
        out[x, :, depth : 2 * depth] = grad.astype(BF16)


def sum_kernel(parts, mixed, grad):
    depth = mixed.shape[1]
    total = parts[0].astype(F32)
    for i in range(1, parts.shape[0]):
        total = total + parts[i].astype(F32)
    mixed[...] = total[:, :depth].astype(BF16)
    grad[...] = total[:, depth:].astype(BF16)


def along_z(x, shift):
    pairs = [(2 * z + c, 2 * ((z + shift * (1 - 2 * c)) % 16) + c) for z in range(16) for c in range(2)]
    return lax.ppermute(x, Z + ("core",), pairs)


def exchange(x):
    return tuple(along_z(x[i], shift) for i, shift in enumerate((1, -1, 2)))


def shards(tokens, grad_out, gate, up, down, gate_scales, up_scales, down_scales):
    n_tok, depth = tokens.shape
    half = gate.shape[1] // (2 * BLK)
    chunks = ((0, (half + 1) // 2), ((half + 1) // 2, half // 2))

    def scaled(kept, chunks, limit, copies=1):
        w = sum(count for _, count in chunks) * BLK
        outs = call(
            functools.partial(scale_kernel, kept, chunks, copies),
            [((3 * depth, count * BLK), BF16) for _, count in chunks] * copies,
            (gate_scales, up_scales, down_scales.T, gate, up, down),
            "scaled",
            specs=[ANY] * 6,
            scratch=[pltpu.VMEM((depth, w), BF16)] * 2
            + [pltpu.VMEM((w, depth), BF16)]
            + [pltpu.SMEM(gate_scales.shape, F32)] * 3
            + [pltpu.SemaphoreType.DMA((6,))],
            limit=limit,
        )
        return outs[: len(chunks)], outs[len(chunks) :]

    def swap(x):
        return lax.ppermute(x, "xl", [(0, 1), (1, 0)])

    (first, second), _ = scaled(False, chunks, 60)
    keeps, _ = scaled(True, chunks, 60)
    first_other = swap(first)
    second, tokens, grad_out = lax.optimization_barrier((second, tokens, grad_out))
    acts = jnp.stack([tokens, grad_out])
    acts = lax.all_to_all(
        jnp.broadcast_to(acts[None], (32,) + acts.shape), ("xl",) + TP, 0, 0, tiled=True
    ).reshape(2, 16, 2, n_tok, depth)
    first_other, second, keeps = lax.optimization_barrier((first_other, second, keeps))
    others = (first_other, swap(second))

    n = 4 * n_tok
    widths = tuple(count * BLK for _, count in chunks)
    w = 3 * sum(widths)
    weights, windows = [], []
    for keep, other, width in zip(keeps, others, widths):
        ins = (acts, keep, other, *windows[1:2])
        *parts, own = call(
            functools.partial(partial_kernel, width),
            [((n, 3 * width), BF16)] * 3 + [((n, 3 * width), F32)],
            ins,
            "partials",
            specs=[VMEM] + [ANY] * (len(ins) - 1),
            scratch=[pltpu.VMEM(keep.shape, BF16)] * 2 + [pltpu.SemaphoreType.DMA((2,))],
        )
        windows += [own, *exchange(parts)]
        weights += [keep, other]
    here, ahead, far, behind = call(
        window_kernel,
        [((n_tok, w), F32)] * 2 + [((n_tok, w), BF16)] * 2,
        windows,
        "window",
        scratch=[pltpu.VMEM((n, w), F32)],
    )
    passed = along_z(far, 4)
    direct = along_z(behind, -4)
    passed = along_z((ahead + passed.astype(F32)).astype(BF16), 4)
    (mine,) = call(
        functools.partial(gated_kernel, widths), [((n_tok, w), BF16)], (here, direct, passed), "gated"
    )
    one, three = along_z(mine, 4), along_z(mine, -4)
    mine = jnp.concatenate([mine, one, along_z(one, 4), three])
    (shares,) = call(
        functools.partial(output_kernel, widths),
        [((2, 16 * n_tok, 2 * depth), BF16)],
        (mine, *exchange([mine] * 3), *weights),
        "outputs",
        scratch=[pltpu.VMEM((4 * n, w), BF16)],
    )
    gathered = lax.all_to_all(
        shares.reshape(32, n_tok, 2 * depth), ("xl",) + TP, 0, 0, tiled=True
    )
    return tuple(call(sum_kernel, [((n_tok, depth), BF16)] * 2, (gathered,), "sums"))


def solution(mesh):
    fine = Mesh(mesh.devices.reshape(4, 4, 2, 2, 4, 2), ("zh", "zl", "xl", "xh", "y", "core"))
    weights, acts = P(SEQ, TP), P(TP, SEQ)
    return jax.shard_map(
        shards,
        mesh=fine,
        in_specs=(acts, acts, weights, weights, acts, weights, weights, acts),
        out_specs=(acts, acts),
        check_vma=False,
    )
```

```python
import functools

import jax
import jax.numpy as jnp
from jax import lax
from jax.experimental import pallas as pl
from jax.experimental.pallas import tpu as pltpu
from jax.sharding import Mesh, PartitionSpec as P

BLK = 128
Z = ("zh", "zl")
TP = ("xh", "y", "core")
SEQ = ("zh", "zl", "xl")
F32, BF16 = jnp.float32, jnp.bfloat16
VMEM = pl.BlockSpec(memory_space=pltpu.VMEM)
SMEM = pl.BlockSpec(memory_space=pltpu.SMEM)
ANY = pl.BlockSpec(memory_space=pl.ANY)


def call(body, out_shapes, ins, name, specs=None, scratch=(), limit=16):
    return pl.pallas_call(
        body,
        out_shape=[jax.ShapeDtypeStruct(s, d) for s, d in out_shapes],
        in_specs=specs or [VMEM] * len(ins),
        out_specs=[VMEM] * len(out_shapes),
        scratch_shapes=list(scratch),
        compiler_params=pltpu.CompilerParams(vmem_limit_bytes=limit * 1024 * 1024),
        name=name,
    )(*ins)


def scale_kernel(kept, chunks, repeats, *refs):
    scales, (gate, up, down) = refs[:3], refs[3:6]
    outs, (g_buf, u_buf, d_buf), tables = refs[6:-7], refs[-7:-4], refs[-4:-1]
    sems = refs[-1]
    depth = g_buf.shape[0]
    half = gate.shape[1] // (2 * BLK)
    xl = lax.axis_index("xl")
    start = (xl if kept else 1 - xl) * half
    lo, count = chunks[0][0], sum(c for _, c in chunks)
    at = pl.ds(pl.multiple_of((start + lo) * BLK, BLK), count * BLK)
    pairs = [(down.at[at, :], d_buf), (gate.at[:, at], g_buf), (up.at[:, at], u_buf)]
    pairs = list(zip(scales, tables)) + pairs
    copies = [pltpu.make_async_copy(a, b, sems.at[i]) for i, (a, b) in enumerate(pairs)]
    for copy in copies[3:] + copies[:3]:
        copy.start()
    for copy in copies[:3]:
        copy.wait()
    gs, us, ds = tables
    for which, copy in enumerate(copies[3:]):
        copy.wait()
        for (first, n), *out in zip(chunks, *(outs[r * len(chunks) :] for r in range(repeats))):
            for j in range(first, first + n):
                src = slice((j - lo) * BLK, (j - lo + 1) * BLK)
                cols = slice((j - first) * BLK, (j - first + 1) * BLK)
                for i in range(depth // BLK):
                    rows = slice(i * BLK, (i + 1) * BLK)
                    if which == 0:
                        to = slice(2 * depth + i * BLK, 2 * depth + (i + 1) * BLK)
                        value = (d_buf[src, rows].astype(F32) * ds[i, start + j]).T
                    elif which == 1:
                        to = rows
                        value = g_buf[rows, src].astype(F32) * gs[i, start + j]
                    else:
                        to = slice(depth + i * BLK, depth + (i + 1) * BLK)
                        value = u_buf[rows, src].astype(F32) * us[i, start + j]
                    for ref in out:
                        ref[to, cols] = value.astype(BF16)


def nt(a, b):
    return lax.dot_general(a, b, (((1,), (1,)), ((), ())), preferred_element_type=F32)


def nn(a, b):
    return jnp.dot(a, b, preferred_element_type=F32)


def toward():
    return 1 - 2 * lax.axis_index("core")


def partial_kernel(width, acts, keep_in, other_in, *refs):
    ahead, behind, far, own, keep, other, sems = refs[-7:]
    copies = [
        pltpu.make_async_copy(keep_in, keep, sems.at[0]),
        pltpu.make_async_copy(other_in, other, sems.at[1]),
    ]
    for copy in copies:
        copy.start()
    for copy in copies:
        copy.wait()
    xl, zl, turn = lax.axis_index("xl"), lax.axis_index("zl"), toward()
    depth = keep.shape[0] // 3
    for shift, out in ((turn, ahead), (-turn, behind), (2, far), (0, own)):
        cls = lax.rem(zl + shift + 4, 4)

        def rows(x, which):
            return jnp.concatenate([acts[x, ch * 4 + cls, which] for ch in range(4)], axis=0)

        for which, ks in ((0, (0, 1)), (1, (2,))):
            mine, his = rows(xl, which), rows(1 - xl, which)
            for k in ks:
                w = slice(k * depth, (k + 1) * depth)
                part = nn(mine, keep[w]) + nn(his, other[w])
                out[:, k * width : (k + 1) * width] = part.astype(out.dtype)


def window_kernel(*refs):
    here, ahead, far, behind, buf = refs[-5:]
    zh, turn = lax.axis_index("zh"), toward()
    n, left = here.shape[0], 0
    for k in range(0, len(refs) - 5, 4):
        own, *parts = refs[k : k + 4]
        total = own[...]
        for part in parts:
            total = total + part[...].astype(F32)
        buf[:, left : left + own.shape[1]] = total
        left += own.shape[1]
    for shift, out in ((2, far), (-turn, behind), (turn, ahead), (0, here)):
        at = pl.ds(pl.multiple_of(lax.rem(zh + shift + 4, 4) * n, n), n)
        out[...] = buf[at, :].astype(out.dtype)


def spans(widths):
    left, at = 0, []
    for w in widths:
        at.append([slice(left + k * w, left + (k + 1) * w) for k in range(3)])
        left += 3 * w
    return at


def gated_kernel(widths, here, direct, passed, out):
    def total(cols):
        return here[:, cols] + direct[:, cols].astype(F32) + passed[:, cols].astype(F32)

    for at in spans(widths):
        gate_sum, up_sum, back_sum = (total(cols) for cols in at)
        sig = jax.nn.sigmoid(gate_sum)
        active = gate_sum * sig
        results = (
            active * up_sum,
            back_sum * up_sum * (sig * (1.0 + gate_sum * (1.0 - sig))),
            back_sum * active,
        )
        for cols, result in zip(at, results):
            out[:, cols] = result.astype(BF16)


def output_kernel(widths, own, ahead, behind, far, *refs):
    weights, out, rows = refs[:-2], refs[-2], refs[-1]
    xl, turn = lax.axis_index("xl"), toward()
    z = lax.axis_index("zh") * 4 + lax.axis_index("zl")
    n = out.shape[1] // 16
    depth = weights[0].shape[0] // 3
    for shift, src in ((0, own), (-turn, ahead), (turn, behind), (-2 * turn, far)):
        sender = lax.rem(z + shift + 16, 16)
        for i, step in enumerate((0, -turn, 2, turn)):
            block = lax.rem(lax.div(sender, 4) + step + 4, 4) * 4 + lax.rem(sender, 4)
            at = pl.ds(pl.multiple_of(block * n, n), n)
            rows[at, :] = src[i * n : (i + 1) * n, :]
    for k, x in enumerate((xl, 1 - xl)):
        mixed = grad = 0.0
        for c, at in enumerate(spans(widths)):
            w = weights[2 * c + k]
            hidden, gate_grad, up_grad = (rows[:, cols] for cols in at)
            mixed = mixed + nt(hidden, w[2 * depth :])
            grad = grad + nt(gate_grad, w[:depth]) + nt(up_grad, w[depth : 2 * depth])
        out[x, :, 0:depth] = mixed.astype(BF16)
        out[x, :, depth : 2 * depth] = grad.astype(BF16)


def sum_kernel(parts, mixed, grad):
    depth = mixed.shape[1]
    total = parts[0].astype(F32)
    for i in range(1, parts.shape[0]):
        total = total + parts[i].astype(F32)
    mixed[...] = total[:, :depth].astype(BF16)
    grad[...] = total[:, depth:].astype(BF16)


def along_z(x, shift):
    pairs = [(2 * z + c, 2 * ((z + shift * (1 - 2 * c)) % 16) + c) for z in range(16) for c in range(2)]
    return lax.ppermute(x, Z + ("core",), pairs)


def exchange(x):
    return tuple(along_z(x[i], shift) for i, shift in enumerate((1, -1, 2)))


def shards(tokens, grad_out, gate, up, down, gate_scales, up_scales, down_scales):
    n_tok, depth = tokens.shape
    half = gate.shape[1] // (2 * BLK)
    chunks = ((0, (half + 1) // 2), ((half + 1) // 2, half // 2))

    def scaled(kept, chunks, limit, copies=1):
        w = sum(count for _, count in chunks) * BLK
        outs = call(
            functools.partial(scale_kernel, kept, chunks, copies),
            [((3 * depth, count * BLK), BF16) for _, count in chunks] * copies,
            (gate_scales, up_scales, down_scales.T, gate, up, down),
            "scaled",
            specs=[ANY] * 6,
            scratch=[pltpu.VMEM((depth, w), BF16)] * 2
            + [pltpu.VMEM((w, depth), BF16)]
            + [pltpu.SMEM(gate_scales.shape, F32)] * 3
            + [pltpu.SemaphoreType.DMA((6,))],
            limit=limit,
        )
        return outs[: len(chunks)], outs[len(chunks) :]

    def swap(x):
        return lax.ppermute(x, "xl", [(0, 1), (1, 0)])

    (first, second), _ = scaled(False, chunks, 60)
    keeps, _ = scaled(True, chunks, 60)
    first_other = swap(first)
    second, tokens, grad_out = lax.optimization_barrier((second, tokens, grad_out))
    acts = jnp.stack([tokens, grad_out])
    acts = lax.all_to_all(
        jnp.broadcast_to(acts[None], (32,) + acts.shape), ("xl",) + TP, 0, 0, tiled=True
    ).reshape(2, 16, 2, n_tok, depth)
    first_other, keeps = lax.optimization_barrier((first_other, keeps))
    other = first_other

    n = 4 * n_tok
    widths = tuple(count * BLK for _, count in chunks)
    w = 3 * sum(widths)
    weights, windows = [], []
    for keep, width in zip(keeps, widths):
        ins = (acts, keep, other, *windows[1:2])
        *parts, own = call(
            functools.partial(partial_kernel, width),
            [((n, 3 * width), BF16)] * 3 + [((n, 3 * width), F32)],
            ins,
            "partials",
            specs=[VMEM] + [ANY] * (len(ins) - 1),
            scratch=[pltpu.VMEM(keep.shape, BF16)] * 2 + [pltpu.SemaphoreType.DMA((2,))],
        )
        weights += [keep, other]
        if len(weights) < 2 * len(widths):
            own, second = lax.optimization_barrier((own, second))
            other = swap(second)
        windows += [own, *exchange(parts)]
    here, ahead, far, behind = call(
        window_kernel,
        [((n_tok, w), F32)] * 2 + [((n_tok, w), BF16)] * 2,
        windows,
        "window",
        scratch=[pltpu.VMEM((n, w), F32)],
    )
    passed = along_z(far, 4)
    direct = along_z(behind, -4)
    passed = along_z((ahead + passed.astype(F32)).astype(BF16), 4)
    (mine,) = call(
        functools.partial(gated_kernel, widths), [((n_tok, w), BF16)], (here, direct, passed), "gated"
    )
    one, three = along_z(mine, 4), along_z(mine, -4)
    mine = jnp.concatenate([mine, one, along_z(one, 4), three])
    (shares,) = call(
        functools.partial(output_kernel, widths),
        [((2, 16 * n_tok, 2 * depth), BF16)],
        (mine, *exchange([mine] * 3), *weights),
        "outputs",
        scratch=[pltpu.VMEM((4 * n, w), BF16)],
    )
    gathered = lax.all_to_all(
        shares.reshape(32, n_tok, 2 * depth), ("xl",) + TP, 0, 0, tiled=True
    )
    return tuple(call(sum_kernel, [((n_tok, depth), BF16)] * 2, (gathered,), "sums"))


def solution(mesh):
    fine = Mesh(mesh.devices.reshape(4, 4, 2, 2, 4, 2), ("zh", "zl", "xl", "xh", "y", "core"))
    weights, acts = P(SEQ, TP), P(TP, SEQ)
    return jax.shard_map(
        shards,
        mesh=fine,
        in_specs=(acts, acts, weights, weights, acts, weights, weights, acts),
        out_specs=(acts, acts),
        check_vma=False,
    )
```

```python
import functools

import jax
import jax.numpy as jnp
from jax import lax
from jax.experimental import pallas as pl
from jax.experimental.pallas import tpu as pltpu
from jax.sharding import Mesh, PartitionSpec as P

BLK = 128
Z = ("zh", "zl")
TP = ("xh", "y", "core")
SEQ = ("zh", "zl", "xl")
F32, BF16 = jnp.float32, jnp.bfloat16
VMEM = pl.BlockSpec(memory_space=pltpu.VMEM)
SMEM = pl.BlockSpec(memory_space=pltpu.SMEM)
ANY = pl.BlockSpec(memory_space=pl.ANY)


def call(body, out_shapes, ins, name, specs=None, scratch=(), limit=16):
    return pl.pallas_call(
        body,
        out_shape=[jax.ShapeDtypeStruct(s, d) for s, d in out_shapes],
        in_specs=specs or [VMEM] * len(ins),
        out_specs=[VMEM] * len(out_shapes),
        scratch_shapes=list(scratch),
        compiler_params=pltpu.CompilerParams(vmem_limit_bytes=limit * 1024 * 1024),
        name=name,
    )(*ins)


def scale_kernel(kept, chunks, repeats, *refs):
    scales, (gate, up, down) = refs[:3], refs[3:6]
    outs, (g_buf, u_buf, d_buf), tables = refs[6:-7], refs[-7:-4], refs[-4:-1]
    sems = refs[-1]
    depth = g_buf.shape[0]
    half = gate.shape[1] // (2 * BLK)
    xl = lax.axis_index("xl")
    start = (xl if kept else 1 - xl) * half
    lo, count = chunks[0][0], sum(c for _, c in chunks)
    at = pl.ds(pl.multiple_of((start + lo) * BLK, BLK), count * BLK)
    pairs = [(down.at[at, :], d_buf), (gate.at[:, at], g_buf), (up.at[:, at], u_buf)]
    pairs = list(zip(scales, tables)) + pairs
    copies = [pltpu.make_async_copy(a, b, sems.at[i]) for i, (a, b) in enumerate(pairs)]
    for copy in copies[3:] + copies[:3]:
        copy.start()
    for copy in copies[:3]:
        copy.wait()
    gs, us, ds = tables
    for which, copy in enumerate(copies[3:]):
        copy.wait()
        for (first, n), *out in zip(chunks, *(outs[r * len(chunks) :] for r in range(repeats))):
            for j in range(first, first + n):
                src = slice((j - lo) * BLK, (j - lo + 1) * BLK)
                cols = slice((j - first) * BLK, (j - first + 1) * BLK)
                for i in range(depth // BLK):
                    rows = slice(i * BLK, (i + 1) * BLK)
                    if which == 0:
                        to = slice(2 * depth + i * BLK, 2 * depth + (i + 1) * BLK)
                        value = (d_buf[src, rows].astype(F32) * ds[i, start + j]).T
                    elif which == 1:
                        to = rows
                        value = g_buf[rows, src].astype(F32) * gs[i, start + j]
                    else:
                        to = slice(depth + i * BLK, depth + (i + 1) * BLK)
                        value = u_buf[rows, src].astype(F32) * us[i, start + j]
                    for ref in out:
                        ref[to, cols] = value.astype(BF16)


def nt(a, b):
    return lax.dot_general(a, b, (((1,), (1,)), ((), ())), preferred_element_type=F32)


def nn(a, b):
    return jnp.dot(a, b, preferred_element_type=F32)


def toward():
    return 1 - 2 * lax.axis_index("core")


def partial_kernel(width, acts, keep_in, other_in, *refs):
    ahead, behind, far, own, keep, other, sems = refs[-7:]
    copies = [
        pltpu.make_async_copy(keep_in, keep, sems.at[0]),
        pltpu.make_async_copy(other_in, other, sems.at[1]),
    ]
    for copy in copies:
        copy.start()
    for copy in copies:
        copy.wait()
    xl, zl, turn = lax.axis_index("xl"), lax.axis_index("zl"), toward()
    depth = keep.shape[0] // 3
    for shift, out in ((turn, ahead), (-turn, behind), (2, far), (0, own)):
        cls = lax.rem(zl + shift + 4, 4)

        def rows(x, which):
            return jnp.concatenate([acts[x, ch * 4 + cls, which] for ch in range(4)], axis=0)

        for which, ks in ((0, (0, 1)), (1, (2,))):
            mine, his = rows(xl, which), rows(1 - xl, which)
            for k in ks:
                w = slice(k * depth, (k + 1) * depth)
                part = nn(mine, keep[w]) + nn(his, other[w])
                out[:, k * width : (k + 1) * width] = part.astype(out.dtype)


def window_kernel(*refs):
    here, ahead, far, behind, buf = refs[-5:]
    zh, turn = lax.axis_index("zh"), toward()
    n, left = here.shape[0], 0
    for k in range(0, len(refs) - 5, 4):
        own, *parts = refs[k : k + 4]
        total = own[...]
        for part in parts:
            total = total + part[...].astype(F32)
        buf[:, left : left + own.shape[1]] = total
        left += own.shape[1]
    for shift, out in ((2, far), (-turn, behind), (turn, ahead), (0, here)):
        at = pl.ds(pl.multiple_of(lax.rem(zh + shift + 4, 4) * n, n), n)
        out[...] = buf[at, :].astype(out.dtype)


def spans(widths):
    left, at = 0, []
    for w in widths:
        at.append([slice(left + k * w, left + (k + 1) * w) for k in range(3)])
        left += 3 * w
    return at


def gated_kernel(widths, here, direct, passed, out):
    def total(cols):
        return here[:, cols] + direct[:, cols].astype(F32) + passed[:, cols].astype(F32)

    for at in spans(widths):
        gate_sum, up_sum, back_sum = (total(cols) for cols in at)
        sig = jax.nn.sigmoid(gate_sum)
        active = gate_sum * sig
        results = (
            active * up_sum,
            back_sum * up_sum * (sig * (1.0 + gate_sum * (1.0 - sig))),
            back_sum * active,
        )
        for cols, result in zip(at, results):
            out[:, cols] = result.astype(BF16)


def output_kernel(widths, own, ahead, behind, far, *refs):
    weights, out, rows = refs[:-2], refs[-2], refs[-1]
    xl, turn = lax.axis_index("xl"), toward()
    z = lax.axis_index("zh") * 4 + lax.axis_index("zl")
    n = out.shape[1] // 16
    depth = weights[0].shape[0] // 3
    for shift, src in ((0, own), (-turn, ahead), (turn, behind), (-2 * turn, far)):
        sender = lax.rem(z + shift + 16, 16)
        for i, step in enumerate((0, -turn, 2, turn)):
            block = lax.rem(lax.div(sender, 4) + step + 4, 4) * 4 + lax.rem(sender, 4)
            at = pl.ds(pl.multiple_of(block * n, n), n)
            rows[at, :] = src[i * n : (i + 1) * n, :]
    for k, x in enumerate((xl, 1 - xl)):
        mixed = grad = 0.0
        for c, at in enumerate(spans(widths)):
            w = weights[2 * c + k]
            hidden, gate_grad, up_grad = (rows[:, cols] for cols in at)
            mixed = mixed + nt(hidden, w[2 * depth :])
            grad = grad + nt(gate_grad, w[:depth]) + nt(up_grad, w[depth : 2 * depth])
        out[x, :, 0:depth] = mixed.astype(BF16)
        out[x, :, depth : 2 * depth] = grad.astype(BF16)


def sum_kernel(parts, mixed, grad):
    depth = mixed.shape[1]
    total = parts[0].astype(F32)
    for i in range(1, parts.shape[0]):
        total = total + parts[i].astype(F32)
    mixed[...] = total[:, :depth].astype(BF16)
    grad[...] = total[:, depth:].astype(BF16)


def along_z(x, shift):
    pairs = [(2 * z + c, 2 * ((z + shift * (1 - 2 * c)) % 16) + c) for z in range(16) for c in range(2)]
    return lax.ppermute(x, Z + ("core",), pairs)


def exchange(x):
    return tuple(along_z(x[i], shift) for i, shift in enumerate((1, -1, 2)))


def shards(tokens, grad_out, gate, up, down, gate_scales, up_scales, down_scales):
    n_tok, depth = tokens.shape
    half = gate.shape[1] // (2 * BLK)
    chunks = ((0, (half + 1) // 2), ((half + 1) // 2, half // 2))

    def scaled(kept, chunks, limit, copies=1):
        w = sum(count for _, count in chunks) * BLK
        outs = call(
            functools.partial(scale_kernel, kept, chunks, copies),
            [((3 * depth, count * BLK), BF16) for _, count in chunks] * copies,
            (gate_scales, up_scales, down_scales.T, gate, up, down),
            "scaled",
            specs=[ANY] * 6,
            scratch=[pltpu.VMEM((depth, w), BF16)] * 2
            + [pltpu.VMEM((w, depth), BF16)]
            + [pltpu.SMEM(gate_scales.shape, F32)] * 3
            + [pltpu.SemaphoreType.DMA((6,))],
            limit=limit,
        )
        return outs[: len(chunks)], outs[len(chunks) :]

    def swap(x):
        return lax.ppermute(x, "xl", [(0, 1), (1, 0)])

    (first, second), _ = scaled(False, chunks, 60)
    keeps, _ = scaled(True, chunks, 60)
    first_other = swap(first)
    second, tokens, grad_out = lax.optimization_barrier((second, tokens, grad_out))
    acts = jnp.stack([tokens, grad_out])
    acts = lax.all_to_all(
        jnp.broadcast_to(acts[None], (32,) + acts.shape), ("xl",) + TP, 0, 0, tiled=True
    ).reshape(2, 16, 2, n_tok, depth)
    first_other, keeps = lax.optimization_barrier((first_other, keeps))
    others = (first_other, swap(second))

    n = 4 * n_tok
    widths = tuple(count * BLK for _, count in chunks)
    w = 3 * sum(widths)
    weights, windows = [], []
    for keep, other, width in zip(keeps, others, widths):
        ins = (acts, keep, other, *windows[1:2])
        *parts, own = call(
            functools.partial(partial_kernel, width),
            [((n, 3 * width), BF16)] * 3 + [((n, 3 * width), F32)],
            ins,
            "partials",
            specs=[VMEM] + [ANY] * (len(ins) - 1),
            scratch=[pltpu.VMEM(keep.shape, BF16)] * 2 + [pltpu.SemaphoreType.DMA((2,))],
        )
        windows += [own, *exchange(parts)]
        weights += [keep, other]
    here, ahead, far, behind = call(
        window_kernel,
        [((n_tok, w), F32)] * 2 + [((n_tok, w), BF16)] * 2,
        windows,
        "window",
        scratch=[pltpu.VMEM((n, w), F32)],
    )
    passed = along_z(far, 4)
    direct = along_z(behind, -4)
    passed = along_z((ahead + passed.astype(F32)).astype(BF16), 4)
    (mine,) = call(
        functools.partial(gated_kernel, widths), [((n_tok, w), BF16)], (here, direct, passed), "gated"
    )
    one, three = along_z(mine, 4), along_z(mine, -4)
    mine = jnp.concatenate([mine, one, along_z(one, 4), three])
    (shares,) = call(
        functools.partial(output_kernel, widths),
        [((2, 16 * n_tok, 2 * depth), BF16)],
        (mine, *exchange([mine] * 3), *weights),
        "outputs",
        scratch=[pltpu.VMEM((4 * n, w), BF16)],
    )
    gathered = lax.all_to_all(
        shares.reshape(32, n_tok, 2 * depth), ("xl",) + TP, 0, 0, tiled=True
    )
    return tuple(call(sum_kernel, [((n_tok, depth), BF16)] * 2, (gathered,), "sums"))


def solution(mesh):
    fine = Mesh(mesh.devices.reshape(4, 4, 2, 2, 4, 2), ("zh", "zl", "xl", "xh", "y", "core"))
    weights, acts = P(SEQ, TP), P(TP, SEQ)
    return jax.shard_map(
        shards,
        mesh=fine,
        in_specs=(acts, acts, weights, weights, acts, weights, weights, acts),
        out_specs=(acts, acts),
        check_vma=False,
    )
```
